256 devices in a mesh: seq: 32 (over x, z), tp: 8 (over y, core).
Axes of the slice: x: 4, y: 4, z: 8, core: 2. Of those that a mesh axis runs over, the one named last changes fastest.
Arguments:
- global_out: bfloat16 [4096, 8192], P('seq', 'tp'), may hold values from -6 to 6
- in_nibbles: int32 [2, 4096, 8], P(None, ('seq', 'tp')), may hold values from 0 to 15
- target_nibbles: int32 [2, 4096, 8], P(None, ('seq', 'tp')), may hold values from 0 to 15
- proj_weight: bfloat16 [1024, 768], replicated, may hold values from -0.1875 to 0.1875
- attn_weight: bfloat16 [4, 768, 768], replicated, may hold values from -0.21875 to 0.21875
- head_weight: bfloat16 [768, 32], replicated, may hold values from -0.625 to 0.625
- byte_embed: bfloat16 [32, 768], replicated, may hold values from -6 to 6
- lo_table: float32 [16, 16], replicated, may hold values from -6 to 6
Outputs:
- grad_global: bfloat16 [4096, 8192], P('seq', 'tp')
- grad_proj: float32 [1024, 768], P(('seq', 'tp'))
- grad_attn: float32 [589824], P(('seq', 'tp'))
- grad_head: float32 [768, 32], replicated
- grad_embed: float32 [32, 768], replicated
- grad_table: float32 [16, 16], replicated
- mean_loss: float32 [], replicated
The draws below stay inside these ranges and needn't reach their ends.
All inputs are finite; a program needn't handle non-finite values.
Results may differ from the reference program's by a relative error of at most 0.012.
Values may be sent and summed in bfloat16 or wider, within the bound.
No kernel may reach another device: no remote copies, remote signals or barrier semaphores. Data moves between devices by JAX's collectives and lax.ppermute only.
A program may use at most 64 MiB of HBM per device.

```python
import jax
import jax.numpy as jnp
from jax import lax

D = 768
DG = 8192
HEADS = 12
HS = 64
K = 8
NIB = 16
PDEV = 16
DGT = 1024
PATCHES = 4096
N_SEQ = 32
N_TP = 8


def with_ends(drawn, stream_key, smallest, largest):
    extent = drawn.shape
    index_at = [jax.random.randint(jax.random.fold_in(stream_key, axis), (), 0, extent[axis]) for axis in range(len(extent))]
    drawn = drawn.at[tuple(index_at)].set(smallest)
    longest = extent.index(max(extent))
    index_at[longest] = (index_at[longest] + 1) % extent[longest]
    return drawn.at[tuple(index_at)].set(largest)


def level_of(key, shape, pieces, least, high):
    loudness, own = 1.0, jax.random.fold_in(key, 6)
    for position, shards_of in pieces:
        heights = jnp.exp(jax.random.uniform(jax.random.fold_in(own, position), (shards_of,), jnp.float32, least / len(pieces), high / len(pieces)))
        loudness = loudness * jnp.repeat(heights, shape[position] // shards_of).reshape([-1 if axis == position else 1 for axis in range(len(shape))])
    return loudness


def gaussian(rng, extent, scale, bound, cuts=(), kind=jnp.bfloat16):
    array = jax.random.normal(rng, extent, jnp.float32) * scale
    if len(cuts) > 0:
        array = level_of(rng, extent, cuts, -0.22, 0.18) * array
    return jnp.clip(array, min=-bound, max=bound).astype(kind)


def setup_inputs(seed: int = 0) -> dict:
    arg_keys = jax.random.split(jax.random.key(seed), 9)
    global_out = gaussian(arg_keys[0], (PATCHES, DG), 1.0, 6.0, ((0, 32), (1, 8)))
    in_nibbles = with_ends(jax.random.randint(arg_keys[1], (2, PATCHES, K), 0, NIB), jax.random.fold_in(arg_keys[1], 1), 0, NIB - 1).astype(jnp.int32)
    target_nibbles = with_ends(jax.random.randint(arg_keys[2], (2, PATCHES, K), 0, NIB), jax.random.fold_in(arg_keys[2], 1), 0, NIB - 1).astype(jnp.int32)
    proj_weight = gaussian(arg_keys[3], (DGT, D), DGT ** -0.5, 0.1875)
    attn_weight = gaussian(arg_keys[4], (4, D, D), D ** -0.5, 0.21875)
    head_weight = gaussian(arg_keys[5], (D, 2 * NIB), (D // 9) ** -0.5, 0.625)
    byte_embed = gaussian(arg_keys[6], (2 * NIB, D), 1.0, 6.0)
    lo_table = gaussian(arg_keys[7], (NIB, NIB), 1.0, 6.0, (), jnp.float32)
    return dict(global_out=global_out, in_nibbles=in_nibbles, target_nibbles=target_nibbles, proj_weight=proj_weight, attn_weight=attn_weight, head_weight=head_weight, byte_embed=byte_embed, lo_table=lo_table)


norm_eps = 1e-06

def to_low(tensor):
    return lax.optimization_barrier(tensor.astype(jnp.bfloat16))

def inverse_rms(values):
    return lax.rsqrt(lax.optimization_barrier(jnp.mean(values * values, axis=-1, keepdims=True)) + norm_eps)

def norm_backward(values, inverse, upstream):
    summed = lax.optimization_barrier(jnp.sum(upstream * values, axis=-1, keepdims=True)) / values.shape[-1]
    return inverse * (upstream - values * (inverse * inverse) * summed)

def contract_rows(left_side, right_side, precision=None):
    return lax.dot_general(left_side, right_side, (((0,), (0,)), ((), ())), preferred_element_type=jnp.float32, precision=precision)

def contract_cols(left_side, right_side):
    return lax.dot_general(left_side, right_side, (((1,), (1,)), ((), ())), preferred_element_type=jnp.float32)

def softmax_rows(logits):
    shifted = logits - lax.optimization_barrier(jnp.max(logits, axis=-1, keepdims=True))
    exponent = jnp.exp(shifted)
    return exponent / lax.optimization_barrier(jnp.sum(exponent, axis=-1, keepdims=True))

def row_loss(row_logits, onehot):
    row_max = lax.optimization_barrier(jnp.max(row_logits, axis=-1))
    total = lax.optimization_barrier(jnp.sum(jnp.exp(row_logits - row_max[:, None]), axis=-1))
    return row_max + jnp.log(total) - lax.optimization_barrier(jnp.sum(row_logits * onehot, axis=-1))

def local_pass(projected, in_nib, tgt_nib, attn_weight, head_weight, byte_embed, lo_table):
    row_count, feat_width = projected.shape
    nibble = lo_table.shape[0]
    patch_count = row_count // K
    code_list = jnp.arange(2 * nibble, dtype=jnp.int32)
    in_onehot = jnp.logical_or(in_nib[0][:, None] == code_list[None, :], in_nib[1][:, None] + nibble == code_list[None, :]).astype(jnp.bfloat16)
    state_in = projected.astype(jnp.float32) + jnp.dot(in_onehot, byte_embed, preferred_element_type=jnp.float32)
    inv_in = inverse_rms(state_in)
    normed_in = to_low(state_in * inv_in)
    query = to_low(jnp.dot(normed_in, attn_weight[0], preferred_element_type=jnp.float32))
    keys_all = to_low(jnp.dot(normed_in, attn_weight[1], preferred_element_type=jnp.float32))
    values_all = to_low(jnp.dot(normed_in, attn_weight[2], preferred_element_type=jnp.float32))

    def split_heads(tensor):
        return tensor.reshape(patch_count, K, HEADS, HS).astype(jnp.float32)
    query_h = split_heads(query)
    keys_h = split_heads(keys_all)
    values_h = split_heads(values_all)
    score_scale = 1.0 / HS ** 0.5
    scores = jnp.einsum('pqhd,pkhd->phqk', query_h, keys_h) * score_scale
    causal = lax.broadcasted_iota(jnp.int32, (K, K), 0) >= lax.broadcasted_iota(jnp.int32, (K, K), 1)
    scores = jnp.where(causal, scores, -1e+30)
    attn_probs = softmax_rows(scores)
    probs_low = to_low(attn_probs).astype(jnp.float32)
    context = to_low(jnp.einsum('phqk,pkhd->pqhd', probs_low, values_h).reshape(row_count, feat_width))
    state_mid = state_in + jnp.dot(context, attn_weight[3], preferred_element_type=jnp.float32)
    inv_mid = inverse_rms(state_mid)
    normed_mid = to_low(state_mid * inv_mid)
    logits = jnp.dot(normed_mid, head_weight, preferred_element_type=jnp.float32)
    nib_codes = jnp.arange(nibble, dtype=jnp.int32)
    hi_onehot = (tgt_nib[0][:, None] == nib_codes[None, :]).astype(jnp.float32)
    lo_onehot = (tgt_nib[1][:, None] == nib_codes[None, :]).astype(jnp.float32)
    hi_logits = logits[:, :nibble]
    lo_logits = logits[:, nibble:] + jnp.dot(hi_onehot, lo_table, precision=lax.Precision.HIGHEST, preferred_element_type=jnp.float32)
    loss_sum = jnp.sum(row_loss(hi_logits, hi_onehot) + row_loss(lo_logits, lo_onehot))
    grad_hi = softmax_rows(hi_logits) - hi_onehot
    grad_lo = softmax_rows(lo_logits) - lo_onehot
    grad_table = contract_rows(hi_onehot, grad_lo, lax.Precision.HIGHEST)
    grad_logits = to_low(jnp.concatenate([grad_hi, grad_lo], axis=1))
    grad_head = contract_rows(normed_mid, grad_logits)
    grad_mid = norm_backward(state_mid, inv_mid, contract_cols(grad_logits, head_weight))
    grad_mid_low = to_low(grad_mid)
    grad_context = to_low(contract_cols(grad_mid_low, attn_weight[3]))
    grad_ctx_h = split_heads(grad_context)
    grad_probs = jnp.einsum('pqhd,pkhd->phqk', grad_ctx_h, values_h)
    grad_values = to_low(jnp.einsum('phqk,pqhd->pkhd', probs_low, grad_ctx_h).reshape(row_count, feat_width))
    grad_scores = to_low(attn_probs * (grad_probs - lax.optimization_barrier(jnp.sum(grad_probs * attn_probs, axis=-1, keepdims=True))) * score_scale)
    grad_scores_f = grad_scores.astype(jnp.float32)
    grad_query = to_low(jnp.einsum('phqk,pkhd->pqhd', grad_scores_f, keys_h).reshape(row_count, feat_width))
    grad_keys = to_low(jnp.einsum('phqk,pqhd->pkhd', grad_scores_f, query_h).reshape(row_count, feat_width))
    grad_value_weight = contract_rows(normed_in, grad_values)
    grad_normed_in = contract_cols(grad_query, attn_weight[0]) + contract_cols(grad_keys, attn_weight[1]) + contract_cols(grad_values, attn_weight[2])
    grad_in = grad_mid + norm_backward(state_in, inv_in, grad_normed_in)
    grad_embed = contract_rows(in_onehot.astype(jnp.float32), grad_in, lax.Precision.HIGHEST)
    return (loss_sum, to_low(grad_in), grad_value_weight, grad_head, grad_embed, grad_table)

def reference(global_out, in_nibbles, target_nibbles, proj_weight, attn_weight, head_weight, byte_embed, lo_table):
    block_rows = PDEV * N_TP
    pos_width = DG // K
    glob_blocks = global_out.reshape(N_SEQ, block_rows, DG)
    in_blocks = in_nibbles.reshape(2, N_SEQ, block_rows * K).transpose(1, 0, 2)
    tgt_blocks = target_nibbles.reshape(2, N_SEQ, block_rows * K).transpose(1, 0, 2)

    def step_block(running, inputs):
        glob_block, in_block, tgt_block = inputs
        pos_rows = glob_block.reshape(block_rows * K, pos_width)
        projected = to_low(jnp.dot(pos_rows, proj_weight, preferred_element_type=jnp.float32))
        loss_sum, grad_rows, grad_value_weight, grad_head, grad_embed, grad_table = local_pass(projected, in_block, tgt_block, attn_weight, head_weight, byte_embed, lo_table)
        grad_glob = to_low(contract_cols(grad_rows, proj_weight)).reshape(block_rows, DG)
        grad_proj = contract_rows(pos_rows, grad_rows)
        updated = (running[0] + loss_sum, running[1] + grad_proj, running[2] + grad_value_weight, running[3] + grad_head, running[4] + grad_embed, running[5] + grad_table)
        return (updated, grad_glob)
    initial = (jnp.zeros((), jnp.float32), jnp.zeros((pos_width, D), jnp.float32), jnp.zeros((D, D), jnp.float32), jnp.zeros((D, 2 * NIB), jnp.float32), jnp.zeros((2 * NIB, D), jnp.float32), jnp.zeros((NIB, NIB), jnp.float32))
    totals, glob_grads = lax.scan(step_block, initial, (glob_blocks, in_blocks, tgt_blocks))
    mean_loss = totals[0] / (PATCHES * K)
    return (glob_grads.reshape(PATCHES, DG), totals[1], totals[2].reshape(D * D), totals[3], totals[4], totals[5], mean_loss)
```

```python
import jax
import jax.numpy as jnp
from jax import lax
from jax.experimental import pallas as pl
from jax.experimental.pallas import tpu as pltpu
from jax.sharding import Mesh, PartitionSpec as P

HEADS = 12
HS = 64
K = 8
PD = 16
ROWS = K * PD
D = 768
DGT = 1024
NIB = 16
LANES = 128
TILES = D // LANES
EPS = 1e-06
F32 = jnp.float32
BF16 = jnp.bfloat16
NX, NZ, NY, NC = 4, 8, 4, 2
BLK = 64
TOTAL_BYTES = 32768


def mm(a, b):
    return jnp.dot(a, b, preferred_element_type=F32)


def mm_t(a, b):
    return lax.dot_general(a, b, (((1,), (1,)), ((), ())), preferred_element_type=F32)


def tmm(a, b, precision=None):
    return lax.dot_general(
        a, b, (((0,), (0,)), ((), ())), preferred_element_type=F32, precision=precision
    )


def norm_backward(values, inverse, upstream):
    summed = jnp.sum(upstream * values, axis=-1, keepdims=True) / D
    return inverse * (upstream - values * (inverse * inverse) * summed)


def owner_columns(size, piece, core):
    block = NZ * NY * NC * piece
    src = lax.broadcasted_iota(jnp.int32, (size, size), 0)
    dst = lax.broadcasted_iota(jnp.int32, (size, size), 1)
    xb = dst // block
    w = dst - xb * block
    half = w // (block // 2)
    w = w - half * (block // 2)
    y = w // (NZ * piece)
    w = w - y * (NZ * piece)
    z = w // piece
    i = w - z * piece
    c = jnp.where(half == 0, 1 - core, core)
    want = xb * block + z * (NY * NC * piece) + y * (NC * piece) + c * piece + i
    return (src == want).astype(BF16)


def softmax_cols(logits):
    e = jnp.exp(logits - jnp.max(logits, axis=0, keepdims=True))
    return e / jnp.sum(e, axis=0, keepdims=True)


def col_loss(logits, onehot):
    top = jnp.max(logits, axis=0, keepdims=True)
    total = jnp.sum(jnp.exp(logits - top), axis=0, keepdims=True)
    return top + jnp.log(total) - jnp.sum(logits * onehot, axis=0, keepdims=True)


def main_kernel(
    pos_ref, nib_ref, proj_ref, attn_ref, head_ref, embed_ref, lo_ref, send_ref, keep_ref, rows_ref
):
    core = lax.axis_index("c")
    pos = pos_ref[...]
    projected = mm(pos, proj_ref[...]).astype(BF16).astype(F32)
    codes = lax.broadcasted_iota(jnp.int32, (2 * NIB, ROWS), 0)
    in_hot = jnp.logical_or(codes == nib_ref[0:1, :], codes == nib_ref[1:2, :] + NIB).astype(BF16)
    state_in = projected + tmm(in_hot, embed_ref[...])
    inv_in = lax.rsqrt(jnp.mean(state_in * state_in, axis=-1, keepdims=True) + EPS)
    normed_in = (state_in * inv_in).astype(BF16)
    query = mm(normed_in, attn_ref[0]).astype(BF16)
    keys = mm(normed_in, attn_ref[1]).astype(BF16)
    values = mm(normed_in, attn_ref[2]).astype(BF16)

    key_row = lax.broadcasted_iota(jnp.int32, (ROWS, 2 * ROWS), 0)
    query_row = lax.broadcasted_iota(jnp.int32, (ROWS, 2 * ROWS), 1) % ROWS
    allowed = jnp.logical_and(key_row % PD == query_row % PD, key_row <= query_row)
    lane = lax.broadcasted_iota(jnp.int32, (2 * ROWS, LANES), 1)
    part = lax.broadcasted_iota(jnp.int32, (2 * ROWS, LANES), 0)
    own = ((lane // HS) == (part // ROWS)).astype(BF16)

    def two_heads(tile):
        return jnp.concatenate([tile, tile], axis=0) * own

    def stacked(cols):
        return jnp.concatenate([cols[:, :ROWS], cols[:, ROWS:]], axis=0)

    scale = 1.0 / HS**0.5
    probs, probs_low, contexts = [], [], []
    for t in range(TILES):
        cut = slice(t * LANES, (t + 1) * LANES)
        scores = mm_t(keys[:, cut], two_heads(query[:, cut])) * scale
        p = softmax_cols(jnp.where(allowed, scores, -1e30))
        low = p.astype(BF16)
        probs.append(p)
        probs_low.append(low)
        contexts.append(tmm(stacked(low), two_heads(values[:, cut])).astype(BF16))
    context = jnp.concatenate(contexts, axis=1)
    state_mid = state_in + mm(context, attn_ref[3])
    inv_mid = lax.rsqrt(jnp.mean(state_mid * state_mid, axis=-1, keepdims=True) + EPS)
    normed_mid = (state_mid * inv_mid).astype(BF16)

    logits = mm_t(head_ref[...], normed_mid)
    nib_codes = lax.broadcasted_iota(jnp.int32, (NIB, ROWS), 0)
    hi_hot = (nib_codes == nib_ref[2:3, :]).astype(F32)
    lo_hot = (nib_codes == nib_ref[3:4, :]).astype(F32)
    hi_logits = logits[:NIB]
    lo_logits = logits[NIB:] + jnp.dot(
        lo_ref[...], hi_hot, precision=lax.Precision.HIGHEST, preferred_element_type=F32
    )
    loss = col_loss(hi_logits, hi_hot) + col_loss(lo_logits, lo_hot)
    grad_hi = softmax_cols(hi_logits) - hi_hot
    grad_lo = softmax_cols(lo_logits) - lo_hot
    grad_table = lax.dot_general(
        hi_hot,
        jnp.concatenate([grad_lo, jnp.zeros((LANES - NIB, ROWS), F32)], axis=0),
        (((1,), (1,)), ((), ())),
        preferred_element_type=F32,
        precision=lax.Precision.HIGHEST,
    )
    grad_logits = jnp.concatenate([grad_hi, grad_lo], axis=0).astype(BF16)
    grad_head = mm(grad_logits, normed_mid)
    grad_mid = norm_backward(state_mid, inv_mid, tmm(grad_logits, head_ref[...]))
    grad_context = mm_t(grad_mid.astype(BF16), attn_ref[3]).astype(BF16)

    grad_q, grad_k, grad_v = [], [], []
    for t in range(TILES):
        cut = slice(t * LANES, (t + 1) * LANES)
        upstream = two_heads(grad_context[:, cut])
        grad_p = mm_t(values[:, cut], upstream)
        grad_v.append(mm(probs_low[t], upstream).astype(BF16))
        inner = jnp.sum(grad_p * probs[t], axis=0, keepdims=True)
        grad_s = (probs[t] * (grad_p - inner) * scale).astype(BF16)
        grad_k.append(mm(grad_s, two_heads(query[:, cut])).astype(BF16))
        grad_q.append(tmm(stacked(grad_s), two_heads(keys[:, cut])).astype(BF16))
    grad_values = jnp.concatenate(grad_v, axis=1)
    grad_normed = (
        mm_t(jnp.concatenate(grad_q, axis=1), attn_ref[0])
        + mm_t(jnp.concatenate(grad_k, axis=1), attn_ref[1])
        + mm_t(grad_values, attn_ref[2])
    )
    grad_in = grad_mid + norm_backward(state_in, inv_in, grad_normed)
    grad_rows = grad_in.astype(BF16)
    rows_ref[...] = grad_rows
    rest = (grad_in - grad_rows.astype(F32)).astype(BF16)
    grad_embed = mm(in_hot, grad_rows) + mm(in_hot, rest)

    attn_cols = mm(normed_in, owner_columns(D, 3, core)).astype(BF16)
    attn_grad = tmm(attn_cols, grad_values)
    move = owner_columns(256, 4, core)
    tail = jnp.concatenate(
        [
            grad_table[:8],
            grad_table[8:],
            jnp.concatenate([loss, jnp.zeros((7, ROWS), F32)], axis=0),
            jnp.zeros((8, D - 3 * LANES), F32),
        ],
        axis=1,
    )
    small = (
        [grad_head[8 * b : 8 * b + 8] for b in range(4)]
        + [grad_embed[8 * b : 8 * b + 8] for b in range(4)]
        + [tail]
        + [jnp.zeros((8, D), F32)] * 7
    )
    for x in range(NX):
        pos_cols = mm(pos[:, 256 * x : 256 * x + 256], move).astype(BF16)
        proj_grad = tmm(pos_cols, grad_rows)
        for half, out in enumerate((send_ref, keep_ref)):
            for y in range(NY):
                a = 128 * half + 32 * y
                b = 192 * x + 96 * half + 24 * y
                out[NY * x + y] = jnp.concatenate(
                    [proj_grad[a : a + 32], attn_grad[b : b + 24], small[NY * x + y]], axis=0
                ).astype(BF16)


def plane_kernel(in_ref, out_ref):
    total = in_ref[0].astype(F32)
    for s in range(1, NX * NY):
        total = total + in_ref[s].astype(F32)
    pad = jnp.zeros((1, D), F32)
    for z in range(NZ):
        out_ref[z] = jnp.concatenate(
            [total[4 * z : 4 * z + 4], total[32 + 3 * z : 35 + 3 * z], pad, total[56:64]], axis=0
        ).astype(BF16)


def column_kernel(in_ref, proj_ref, attn_ref, small_ref):
    total = in_ref[0].astype(F32)
    for s in range(1, NZ):
        total = total + in_ref[s].astype(F32)
    proj_ref[...] = total[0:4]
    attn_ref[...] = total[4:7]
    mine = total[8:16].astype(BF16)
    for s in range(NX * NY // 2):
        small_ref[s] = jnp.concatenate([mine, mine], axis=0)


def last_kernel(in_ref, head_ref, embed_ref, table_ref, loss_ref):
    got = in_ref[...].astype(F32)
    head_ref[...] = jnp.transpose(got[0:32])
    embed_ref[...] = got[32:64]
    tail = got[64:72]
    table_ref[...] = jnp.concatenate([tail[:, 0:NIB], tail[:, LANES : LANES + NIB]], axis=0)
    loss_ref[...] = jnp.sum(tail[0:1, 2 * LANES : 3 * LANES], axis=1, keepdims=True) / TOTAL_BYTES


def call(kernel, outs, vmem=16 * 1024 * 1024):
    return pl.pallas_call(
        kernel,
        out_shape=[jax.ShapeDtypeStruct(s, d) for s, d in outs],
        compiler_params=pltpu.CompilerParams(vmem_limit_bytes=vmem),
    )


def local(
    global_out, in_nibbles, target_nibbles, proj_weight, attn_weight, head_weight, byte_embed, lo_table
):
    plane = ("x", "y")
    pos = lax.all_to_all(
        global_out.reshape(K, PD, DGT), ("y", "c"), split_axis=0, concat_axis=0, tiled=True
    ).reshape(ROWS, DGT)
    nibbles = jnp.concatenate([in_nibbles, target_nibbles], axis=0)
    nibbles = nibbles.transpose(0, 2, 1).reshape(4, ROWS)
    send, keep, grad_rows = call(
        main_kernel,
        [((16, BLK, D), BF16), ((16, BLK, D), BF16), ((ROWS, D), BF16)],
        48 * 1024 * 1024,
    )(pos, nibbles, proj_weight, attn_weight, head_weight.T, byte_embed, lo_table.T)
    got = lax.ppermute(send, "c", [(0, 1), (1, 0)])
    pair = (got.astype(F32) + keep.astype(F32)).astype(BF16)
    blocks = lax.all_to_all(pair, plane, split_axis=0, concat_axis=0, tiled=True)
    (columns,) = call(plane_kernel, [((NZ, 16, D), BF16)])(blocks)
    columns = lax.all_to_all(columns, "z", split_axis=0, concat_axis=0, tiled=True)
    grad_proj, grad_attn, small = call(
        column_kernel, [((4, D), F32), ((3, D), F32), ((NX * NY // 2, 16, D), BF16)]
    )(columns)
    small = lax.all_to_all(
        small.reshape(NX * NY, 8, D), plane, split_axis=0, concat_axis=0, tiled=True
    )
    grad_head, grad_embed, grad_table, loss = call(
        last_kernel,
        [((D, 2 * NIB), F32), ((2 * NIB, D), F32), ((NIB, NIB), F32), ((1, 1), F32)],
    )(small.reshape(NX * NY * 8, D))

    grad_back = lax.all_to_all(
        grad_rows.reshape(K, PD, D), ("y", "c"), split_axis=0, concat_axis=0, tiled=True
    ).reshape(ROWS, D)
    grad_global = mm_t(grad_back, proj_weight).astype(BF16)
    return (
        grad_global,
        grad_proj,
        grad_attn.reshape(3 * D),
        grad_head,
        grad_embed,
        grad_table,
        loss.reshape(()),
    )


def solution(mesh):
    axes = Mesh(mesh.devices.reshape(NX, NZ, NY, NC), ("x", "z", "y", "c"))
    every = ("x", "z", "y", "c")
    shard = P(("x", "z"), ("y", "c"))
    in_specs = (shard, P(None, every, None), P(None, every, None), P(), P(), P(), P(), P())
    out_specs = (shard, P(every, None), P(every), P(), P(), P(), P())
    return jax.shard_map(local, mesh=axes, in_specs=in_specs, out_specs=out_specs, check_vma=False)
```

```python
import jax
import jax.numpy as jnp
from jax import lax
from jax.experimental import pallas as pl
from jax.experimental.pallas import tpu as pltpu
from jax.sharding import Mesh, PartitionSpec as P

HEADS = 12
HS = 64
K = 8
PD = 16
ROWS = K * PD
D = 768
DGT = 1024
NIB = 16
LANES = 128
TILES = D // LANES
EPS = 1e-06
F32 = jnp.float32
BF16 = jnp.bfloat16
NX, NZ, NY, NC = 4, 8, 4, 2
PLANE = NX * NY
SMALL = 512
BLK = 7 * D + SMALL
GROWS = 336
TOTAL_BYTES = 32768


def mm(a, b):
    return jnp.dot(a, b, preferred_element_type=F32)


def mm_t(a, b):
    return lax.dot_general(a, b, (((1,), (1,)), ((), ())), preferred_element_type=F32)


def tmm(a, b, precision=None):
    return lax.dot_general(
        a, b, (((0,), (0,)), ((), ())), preferred_element_type=F32, precision=precision
    )


def norm_backward(values, inverse, upstream):
    summed = jnp.sum(upstream * values, axis=-1, keepdims=True) / D
    return inverse * (upstream - values * (inverse * inverse) * summed)


def owner_columns(size, piece, core):
    block = NZ * NY * NC * piece
    src = lax.broadcasted_iota(jnp.int32, (size, size), 0)
    dst = lax.broadcasted_iota(jnp.int32, (1, size), 1)
    half = dst // (size // 2)
    w = dst - half * (size // 2)
    xb = w // (block // 2)
    w = w - xb * (block // 2)
    y = w // (NZ * piece)
    w = w - y * (NZ * piece)
    z = w // piece
    i = w - z * piece
    c = jnp.where(half == 0, 1 - core, core)
    want = xb * block + z * (NY * NC * piece) + y * (NC * piece) + c * piece + i
    return (src == want).astype(BF16)


def softmax_cols(logits):
    e = jnp.exp(logits - jnp.max(logits, axis=0, keepdims=True))
    return e / jnp.sum(e, axis=0, keepdims=True)


def col_loss(logits, onehot):
    top = jnp.max(logits, axis=0, keepdims=True)
    total = jnp.sum(jnp.exp(logits - top), axis=0, keepdims=True)
    return top + jnp.log(total) - jnp.sum(logits * onehot, axis=0, keepdims=True)


def fetch_kernel(proj_hbm, proj_ref, sem):
    copy = pltpu.make_async_copy(proj_hbm, proj_ref, sem)
    copy.start()
    copy.wait()


def input_hot(nib_ref):
    codes = lax.broadcasted_iota(jnp.int32, (2 * NIB, ROWS), 0)
    return jnp.logical_or(codes == nib_ref[0:1, :], codes == nib_ref[1:2, :] + NIB).astype(BF16)


def main_kernel(
    pos_ref,
    nib_ref,
    proj_ref,
    embed_ref,
    attn_hbm,
    head_ref,
    lo_ref,
    out_ref,
    send_ref,
    keep_ref,
    attn_ref,
    sems,
):
    copies = [pltpu.make_async_copy(attn_hbm.at[w], attn_ref.at[w], sems.at[w]) for w in range(4)]
    for copy in copies:
        copy.start()
    core = lax.axis_index("c")
    pos = pos_ref[...]
    projected = mm(pos, proj_ref[...]).astype(BF16).astype(F32)
    in_hot = input_hot(nib_ref)
    state_in = projected + tmm(in_hot, embed_ref[...])
    inv_in = lax.rsqrt(jnp.mean(state_in * state_in, axis=-1, keepdims=True) + EPS)
    normed_in = (state_in * inv_in).astype(BF16)
    move = owner_columns(256, 4, core)
    for x in range(NX):
        cols = mm(pos[:, 256 * x : 256 * x + 256], move).astype(BF16)
        send_ref[:, 128 * x : 128 * x + 128] = cols[:, :128]
        keep_ref[:, 128 * x : 128 * x + 128] = cols[:, 128:]
    cols = mm(normed_in, owner_columns(D, 3, core)).astype(BF16)
    send_ref[:, 512:] = cols[:, : D // 2]
    keep_ref[:, 512:] = cols[:, D // 2 :]
    copies[0].wait()
    query = mm(normed_in, attn_ref[0]).astype(BF16)
    copies[1].wait()
    keys = mm(normed_in, attn_ref[1]).astype(BF16)
    copies[2].wait()
    values = mm(normed_in, attn_ref[2]).astype(BF16)

    key_row = lax.broadcasted_iota(jnp.int32, (ROWS, 2 * ROWS), 0)
    query_row = lax.broadcasted_iota(jnp.int32, (ROWS, 2 * ROWS), 1) % ROWS
    allowed = jnp.logical_and(key_row % PD == query_row % PD, key_row <= query_row)
    lane = lax.broadcasted_iota(jnp.int32, (2 * ROWS, LANES), 1)
    part = lax.broadcasted_iota(jnp.int32, (2 * ROWS, LANES), 0)
    own = ((lane // HS) == (part // ROWS)).astype(BF16)

    def two_heads(tile):
        return jnp.concatenate([tile, tile], axis=0) * own

    def stacked(cols):
        return jnp.concatenate([cols[:, :ROWS], cols[:, ROWS:]], axis=0)

    scale = 1.0 / HS**0.5
    probs, probs_low, contexts = [], [], []
    for t in range(TILES):
        cut = slice(t * LANES, (t + 1) * LANES)
        scores = mm_t(keys[:, cut], two_heads(query[:, cut])) * scale
        p = softmax_cols(jnp.where(allowed, scores, -1e30))
        low = p.astype(BF16)
        probs.append(p)
        probs_low.append(low)
        contexts.append(tmm(stacked(low), two_heads(values[:, cut])).astype(BF16))
    context = jnp.concatenate(contexts, axis=1)
    copies[3].wait()
    state_mid = state_in + mm(context, attn_ref[3])
    inv_mid = lax.rsqrt(jnp.mean(state_mid * state_mid, axis=-1, keepdims=True) + EPS)
    normed_mid = (state_mid * inv_mid).astype(BF16)

    logits = mm_t(head_ref[...], normed_mid)
    nib_codes = lax.broadcasted_iota(jnp.int32, (NIB, ROWS), 0)
    hi_hot = (nib_codes == nib_ref[2:3, :]).astype(F32)
    lo_hot = (nib_codes == nib_ref[3:4, :]).astype(F32)
    hi_logits = logits[:NIB]
    lo_logits = logits[NIB:] + jnp.dot(
        lo_ref[...], hi_hot, precision=lax.Precision.HIGHEST, preferred_element_type=F32
    )
    loss = col_loss(hi_logits, hi_hot) + col_loss(lo_logits, lo_hot)
    grad_hi = softmax_cols(hi_logits) - hi_hot
    grad_lo = softmax_cols(lo_logits) - lo_hot
    grad_table = lax.dot_general(
        hi_hot,
        jnp.concatenate([grad_lo, jnp.zeros((LANES - NIB, ROWS), F32)], axis=0),
        (((1,), (1,)), ((), ())),
        preferred_element_type=F32,
        precision=lax.Precision.HIGHEST,
    )
    grad_logits = jnp.concatenate([grad_hi, grad_lo], axis=0).astype(BF16)
    grad_head = mm(grad_logits, normed_mid)
    grad_mid = norm_backward(state_mid, inv_mid, tmm(grad_logits, head_ref[...]))
    grad_context = mm_t(grad_mid.astype(BF16), attn_ref[3]).astype(BF16)

    grad_q, grad_k, grad_v = [], [], []
    for t in range(TILES):
        cut = slice(t * LANES, (t + 1) * LANES)
        upstream = two_heads(grad_context[:, cut])
        grad_p = mm_t(values[:, cut], upstream)
        grad_v.append(mm(probs_low[t], upstream).astype(BF16))
        inner = jnp.sum(grad_p * probs[t], axis=0, keepdims=True)
        grad_s = (probs[t] * (grad_p - inner) * scale).astype(BF16)
        grad_k.append(mm(grad_s, two_heads(query[:, cut])).astype(BF16))
        grad_q.append(tmm(stacked(grad_s), two_heads(keys[:, cut])).astype(BF16))
    grad_values = jnp.concatenate(grad_v, axis=1)
    grad_normed = (
        mm_t(jnp.concatenate(grad_q, axis=1), attn_ref[0])
        + mm_t(jnp.concatenate(grad_k, axis=1), attn_ref[1])
        + mm_t(grad_values, attn_ref[2])
    )
    grad_in = grad_mid + norm_backward(state_in, inv_in, grad_normed)
    grad_rows = grad_in.astype(BF16)
    rest = (grad_in - grad_rows.astype(F32)).astype(BF16)
    grad_embed = mm(in_hot, grad_rows) + mm(in_hot, rest)

    out_ref[0:ROWS] = grad_rows
    out_ref[ROWS : 2 * ROWS] = grad_values
    tail = jnp.concatenate(
        [
            grad_table[:8],
            grad_table[8:],
            jnp.concatenate([loss, jnp.zeros((7, ROWS), F32)], axis=0),
            jnp.zeros((8, D - 3 * LANES), F32),
        ],
        axis=1,
    )
    out_ref[2 * ROWS : GROWS] = jnp.concatenate(
        [grad_head, grad_embed, tail, jnp.zeros((8, D), F32)], axis=0
    ).astype(BF16)


def pair_kernel(ka_ref, ra_ref, kg_ref, rg_ref, out_ref, *back_refs):
    core = lax.axis_index("c")
    y = lax.axis_index("y")
    cols = jnp.concatenate([ka_ref[...], ra_ref[...]], axis=0)
    rows = jnp.concatenate([kg_ref[0:ROWS], rg_ref[0:ROWS]], axis=0)
    values = jnp.concatenate([kg_ref[ROWS : 2 * ROWS], rg_ref[ROWS : 2 * ROWS]], axis=0)
    for d, back in enumerate(back_refs):
        at = pl.ds(pl.multiple_of((2 * lax.rem(y + d, NY) + core) * PD, PD), PD)
        mine, other = kg_ref[at], rg_ref[at]
        first = core == 0
        back[0:PD] = jnp.where(first, mine, other)
        back[PD : 2 * PD] = jnp.where(first, other, mine)
    small = kg_ref[2 * ROWS :].astype(F32) + rg_ref[2 * ROWS :].astype(F32)
    flat = jnp.concatenate(
        [small[8 * g : 8 * g + 8] for g in range(9)] + [jnp.zeros((8, PLANE * SMALL - 9 * D), F32)], axis=1
    ).astype(BF16)
    proj_grad = tmm(cols[:, :512], rows)
    attn_grad = tmm(cols[:, 512:], values)
    for b in range(PLANE):
        groups = [proj_grad[32 * b + 8 * g : 32 * b + 8 * g + 8] for g in range(4)]
        groups += [attn_grad[24 * b + 8 * g : 24 * b + 8 * g + 8] for g in range(3)]
        for g, group in enumerate(groups):
            out_ref[b, :, g * D : (g + 1) * D] = group.astype(BF16)
        out_ref[b, :, 7 * D :] = flat[:, b * SMALL : (b + 1) * SMALL]


def back_kernel(p0_ref, p1_ref, p2_ref, p3_ref, proj_ref, out_ref, rows_ref):
    y = lax.axis_index("y")
    for d, piece in enumerate((p0_ref, p1_ref, p2_ref, p3_ref)):
        at = pl.ds(pl.multiple_of(lax.rem(y - d + NY, NY) * 2 * PD, 2 * PD), 2 * PD)
        rows_ref[at] = piece[...]
    out_ref[...] = mm_t(rows_ref[...], proj_ref[...]).astype(BF16)


def plane_kernel(in_ref, out_ref):
    total = in_ref[0].astype(F32)
    for s in range(1, PLANE):
        total = total + in_ref[s].astype(F32)
    proj = jnp.concatenate([total[:, g * D : (g + 1) * D] for g in range(4)], axis=0)
    attn = jnp.concatenate([total[:, g * D : (g + 1) * D] for g in range(4, 7)], axis=0)
    small = total[:, 7 * D :].astype(BF16)
    pad = jnp.zeros((1, D), F32)
    for z in range(NZ):
        own = jnp.concatenate([proj[4 * z : 4 * z + 4], attn[3 * z : 3 * z + 3], pad], axis=0)
        out_ref[z, :, :D] = own.astype(BF16)
        out_ref[z, :, D:] = small


def column_kernel(in_ref, proj_ref, attn_ref, small_ref):
    total = in_ref[0].astype(F32)
    for s in range(1, NZ):
        total = total + in_ref[s].astype(F32)
    proj_ref[...] = total[0:4, :D]
    attn_ref[...] = total[4:7, :D]
    mine = total[:, D:].astype(BF16)
    for s in range(PLANE):
        small_ref[s] = mine


def last_kernel(in_ref, head_ref, embed_ref, table_ref, loss_ref):
    got = jnp.concatenate([in_ref[b] for b in range(13)], axis=1).astype(F32)
    for g in range(4):
        head_ref[8 * g : 8 * g + 8] = got[:, g * D : (g + 1) * D]
        embed_ref[8 * g : 8 * g + 8] = got[:, (4 + g) * D : (5 + g) * D]
    tail = got[:, 8 * D :]
    table_ref[...] = jnp.concatenate([tail[:, 0:NIB], tail[:, LANES : LANES + NIB]], axis=0)
    loss_ref[...] = jnp.sum(tail[0:1, 2 * LANES : 3 * LANES], axis=1, keepdims=True) / TOTAL_BYTES


def call(kernel, outs, vmem=8, **more):
    return pl.pallas_call(
        kernel,
        out_shape=[jax.ShapeDtypeStruct(s, d) for s, d in outs],
        compiler_params=pltpu.CompilerParams(vmem_limit_bytes=vmem * 1024 * 1024),
        **more,
    )


def local(
    global_out, in_nibbles, target_nibbles, proj_weight, attn_weight, head_weight, byte_embed, lo_table
):
    plane = ("x", "y")
    swap = [(0, 1), (1, 0)]
    pos = lax.all_to_all(
        global_out.reshape(K, PD, DGT), ("y", "c"), split_axis=0, concat_axis=0, tiled=True
    ).reshape(ROWS, DGT)
    nibbles = jnp.concatenate([in_nibbles, target_nibbles], axis=0)
    nibbles = nibbles.transpose(0, 2, 1).reshape(4, ROWS)
    (proj_weight,) = call(
        fetch_kernel,
        [(proj_weight.shape, BF16)],
        in_specs=[pl.BlockSpec(memory_space=pl.ANY)],
        scratch_shapes=[pltpu.SemaphoreType.DMA],
    )(proj_weight)
    half = (ROWS, (DGT + D) // NC)
    local_spec = pl.BlockSpec(memory_space=pltpu.VMEM)
    grads, send_cols, keep_cols = call(
        main_kernel,
        [((GROWS, D), BF16), (half, BF16), (half, BF16)],
        52,
        in_specs=[local_spec] * 4 + [pl.BlockSpec(memory_space=pl.ANY)] + [local_spec] * 2,
        scratch_shapes=[pltpu.VMEM((4, D, D), BF16), pltpu.SemaphoreType.DMA((4,))],
    )(pos, nibbles, proj_weight, byte_embed, attn_weight, head_weight.T, lo_table.T)
    got_cols = lax.ppermute(send_cols, "c", swap)
    got_grads = lax.ppermute(grads, "c", swap)
    blocks, *back = call(pair_kernel, [((PLANE, 8, BLK), BF16)] + [((2 * PD, D), BF16)] * NY, 12)(
        keep_cols, got_cols, grads, got_grads
    )
    blocks = lax.all_to_all(blocks, plane, split_axis=0, concat_axis=0, tiled=True)
    for d in range(1, NY):
        back[d] = lax.ppermute(back[d], "y", [(s, (s + d) % NY) for s in range(NY)])
    (grad_global,) = call(
        back_kernel, [((ROWS, DGT), BF16)], scratch_shapes=[pltpu.VMEM((ROWS, D), BF16)]
    )(*back, proj_weight)
    blocks, grad_global = lax.optimization_barrier((blocks, grad_global))
    (columns,) = call(plane_kernel, [((NZ, 8, D + SMALL), BF16)])(blocks)
    columns = lax.all_to_all(columns, "z", split_axis=0, concat_axis=0, tiled=True)
    grad_proj, grad_attn, small = call(
        column_kernel, [((4, D), F32), ((3, D), F32), ((PLANE, 8, SMALL), BF16)]
    )(columns)
    small = lax.all_to_all(small, plane, split_axis=0, concat_axis=0, tiled=True)
    head_rows, grad_embed, grad_table, loss = call(
        last_kernel,
        [((2 * NIB, D), F32), ((2 * NIB, D), F32), ((NIB, NIB), F32), ((1, 1), F32)],
    )(small)
    return (
        grad_global,
        grad_proj,
        grad_attn.reshape(3 * D),
        head_rows.T,
        grad_embed,
        grad_table,
        loss.reshape(()),
    )


def solution(mesh):
    axes = Mesh(mesh.devices.reshape(NX, NZ, NY, NC), ("x", "z", "y", "c"))
    every = ("x", "z", "y", "c")
    shard = P(("x", "z"), ("y", "c"))
    in_specs = (shard, P(None, every, None), P(None, every, None), P(), P(), P(), P(), P())
    out_specs = (shard, P(every, None), P(every), P(), P(), P(), P())
    return jax.shard_map(local, mesh=axes, in_specs=in_specs, out_specs=out_specs, check_vma=False)
```

```python
import jax
import jax.numpy as jnp
from jax import lax
from jax.experimental import pallas as pl
from jax.experimental.pallas import tpu as pltpu
from jax.sharding import Mesh, PartitionSpec as P

HEADS = 12
HS = 64
K = 8
PD = 16
ROWS = K * PD
D = 768
DGT = 1024
NIB = 16
LANES = 128
TILES = D // LANES
EPS = 1e-06
F32 = jnp.float32
BF16 = jnp.bfloat16
NX, NZ, NY, NC = 4, 8, 4, 2
PLANE = NX * NY
SMALL = 512
BLK = 7 * D + SMALL
GROWS = 336
TOTAL_BYTES = 32768


def mm(a, b):
    return jnp.dot(a, b, preferred_element_type=F32)


def mm_t(a, b):
    return lax.dot_general(a, b, (((1,), (1,)), ((), ())), preferred_element_type=F32)


def tmm(a, b, precision=None):
    return lax.dot_general(
        a, b, (((0,), (0,)), ((), ())), preferred_element_type=F32, precision=precision
    )


def norm_backward(values, inverse, upstream):
    summed = jnp.sum(upstream * values, axis=-1, keepdims=True) / D
    return inverse * (upstream - values * (inverse * inverse) * summed)


def owner_columns(size, piece, core):
    block = NZ * NY * NC * piece
    src = lax.broadcasted_iota(jnp.int32, (size, size), 0)
    dst = lax.broadcasted_iota(jnp.int32, (1, size), 1)
    half = dst // (size // 2)
    w = dst - half * (size // 2)
    xb = w // (block // 2)
    w = w - xb * (block // 2)
    y = w // (NZ * piece)
    w = w - y * (NZ * piece)
    z = w // piece
    i = w - z * piece
    c = jnp.where(half == 0, 1 - core, core)
    want = xb * block + z * (NY * NC * piece) + y * (NC * piece) + c * piece + i
    return (src == want).astype(BF16)


def softmax_cols(logits):
    e = jnp.exp(logits - jnp.max(logits, axis=0, keepdims=True))
    return e / jnp.sum(e, axis=0, keepdims=True)


def col_loss(logits, onehot):
    top = jnp.max(logits, axis=0, keepdims=True)
    total = jnp.sum(jnp.exp(logits - top), axis=0, keepdims=True)
    return top + jnp.log(total) - jnp.sum(logits * onehot, axis=0, keepdims=True)


def fetch_kernel(proj_hbm, proj_ref, sem):
    copy = pltpu.make_async_copy(proj_hbm, proj_ref, sem)
    copy.start()
    copy.wait()


def input_hot(nib_ref):
    codes = lax.broadcasted_iota(jnp.int32, (2 * NIB, ROWS), 0)
    return jnp.logical_or(codes == nib_ref[0:1, :], codes == nib_ref[1:2, :] + NIB).astype(BF16)


def main_kernel(
    pos_ref,
    nib_ref,
    proj_ref,
    embed_ref,
    attn_hbm,
    head_ref,
    lo_ref,
    out_ref,
    send_ref,
    keep_ref,
    attn_ref,
    sems,
):
    copies = [pltpu.make_async_copy(attn_hbm.at[w], attn_ref.at[w], sems.at[w]) for w in range(4)]
    for copy in copies:
        copy.start()
    core = lax.axis_index("c")
    pos = pos_ref[...]
    projected = mm(pos, proj_ref[...]).astype(BF16).astype(F32)
    in_hot = input_hot(nib_ref)
    state_in = projected + tmm(in_hot, embed_ref[...])
    inv_in = lax.rsqrt(jnp.mean(state_in * state_in, axis=-1, keepdims=True) + EPS)
    normed_in = (state_in * inv_in).astype(BF16)
    move = owner_columns(256, 4, core)
    for x in range(NX):
        cols = mm(pos[:, 256 * x : 256 * x + 256], move).astype(BF16)
        send_ref[:, 128 * x : 128 * x + 128] = cols[:, :128]
        keep_ref[:, 128 * x : 128 * x + 128] = cols[:, 128:]
    cols = mm(normed_in, owner_columns(D, 3, core)).astype(BF16)
    send_ref[:, 512:] = cols[:, : D // 2]
    keep_ref[:, 512:] = cols[:, D // 2 :]
    copies[0].wait()
    query = mm(normed_in, attn_ref[0]).astype(BF16)
    copies[1].wait()
    keys = mm(normed_in, attn_ref[1]).astype(BF16)
    copies[2].wait()
    values = mm(normed_in, attn_ref[2]).astype(BF16)

    key_row = lax.broadcasted_iota(jnp.int32, (ROWS, 2 * ROWS), 0)
    query_row = lax.broadcasted_iota(jnp.int32, (ROWS, 2 * ROWS), 1) % ROWS
    allowed = jnp.logical_and(key_row % PD == query_row % PD, key_row <= query_row)
    lane = lax.broadcasted_iota(jnp.int32, (2 * ROWS, LANES), 1)
    part = lax.broadcasted_iota(jnp.int32, (2 * ROWS, LANES), 0)
    own = ((lane // HS) == (part // ROWS)).astype(BF16)

    def two_heads(tile):
        return jnp.concatenate([tile, tile], axis=0) * own

    def stacked(cols):
        return jnp.concatenate([cols[:, :ROWS], cols[:, ROWS:]], axis=0)

    scale = 1.0 / HS**0.5
    probs, probs_low, contexts = [], [], []
    for t in range(TILES):
        cut = slice(t * LANES, (t + 1) * LANES)
        scores = mm_t(keys[:, cut], two_heads(query[:, cut])) * scale
        p = softmax_cols(jnp.where(allowed, scores, -1e30))
        low = p.astype(BF16)
        probs.append(p)
        probs_low.append(low)
        contexts.append(tmm(stacked(low), two_heads(values[:, cut])).astype(BF16))
    context = jnp.concatenate(contexts, axis=1)
    copies[3].wait()
    state_mid = state_in + mm(context, attn_ref[3])
    inv_mid = lax.rsqrt(jnp.mean(state_mid * state_mid, axis=-1, keepdims=True) + EPS)
    normed_mid = (state_mid * inv_mid).astype(BF16)

    logits = mm_t(head_ref[...], normed_mid)
    nib_codes = lax.broadcasted_iota(jnp.int32, (NIB, ROWS), 0)
    hi_hot = (nib_codes == nib_ref[2:3, :]).astype(F32)
    lo_hot = (nib_codes == nib_ref[3:4, :]).astype(F32)
    hi_logits = logits[:NIB]
    lo_logits = logits[NIB:] + jnp.dot(
        lo_ref[...], hi_hot, precision=lax.Precision.HIGHEST, preferred_element_type=F32
    )
    loss = col_loss(hi_logits, hi_hot) + col_loss(lo_logits, lo_hot)
    grad_hi = softmax_cols(hi_logits) - hi_hot
    grad_lo = softmax_cols(lo_logits) - lo_hot
    grad_table = lax.dot_general(
        hi_hot,
        jnp.concatenate([grad_lo, jnp.zeros((LANES - NIB, ROWS), F32)], axis=0),
        (((1,), (1,)), ((), ())),
        preferred_element_type=F32,
        precision=lax.Precision.HIGHEST,
    )
    grad_logits = jnp.concatenate([grad_hi, grad_lo], axis=0).astype(BF16)
    grad_head = mm(grad_logits, normed_mid)
    grad_mid = norm_backward(state_mid, inv_mid, tmm(grad_logits, head_ref[...]))
    grad_context = mm_t(grad_mid.astype(BF16), attn_ref[3]).astype(BF16)

    grad_q, grad_k, grad_v = [], [], []
    for t in range(TILES):
        cut = slice(t * LANES, (t + 1) * LANES)
        upstream = two_heads(grad_context[:, cut])
        grad_p = mm_t(values[:, cut], upstream)
        grad_v.append(mm(probs_low[t], upstream).astype(BF16))
        inner = jnp.sum(grad_p * probs[t], axis=0, keepdims=True)
        grad_s = (probs[t] * (grad_p - inner) * scale).astype(BF16)
        grad_k.append(mm(grad_s, two_heads(query[:, cut])).astype(BF16))
        grad_q.append(tmm(stacked(grad_s), two_heads(keys[:, cut])).astype(BF16))
    grad_values = jnp.concatenate(grad_v, axis=1)
    grad_normed = (
        mm_t(jnp.concatenate(grad_q, axis=1), attn_ref[0])
        + mm_t(jnp.concatenate(grad_k, axis=1), attn_ref[1])
        + mm_t(grad_values, attn_ref[2])
    )
    grad_in = grad_mid + norm_backward(state_in, inv_in, grad_normed)
    grad_rows = grad_in.astype(BF16)
    rest = (grad_in - grad_rows.astype(F32)).astype(BF16)
    grad_embed = mm(in_hot, grad_rows) + mm(in_hot, rest)

    out_ref[0:ROWS] = grad_rows
    out_ref[ROWS : 2 * ROWS] = grad_values
    tail = jnp.concatenate(
        [
            grad_table[:8],
            grad_table[8:],
            jnp.concatenate([loss, jnp.zeros((7, ROWS), F32)], axis=0),
            jnp.zeros((8, D - 3 * LANES), F32),
        ],
        axis=1,
    )
    out_ref[2 * ROWS : GROWS] = jnp.concatenate(
        [grad_head, grad_embed, tail, jnp.zeros((8, D), F32)], axis=0
    ).astype(BF16)


def pair_kernel(ka_ref, ra_ref, kg_ref, rg_ref, out_ref, *back_refs):
    core = lax.axis_index("c")
    y = lax.axis_index("y")
    cols = jnp.concatenate([ka_ref[...], ra_ref[...]], axis=0)
    rows = jnp.concatenate([kg_ref[0:ROWS], rg_ref[0:ROWS]], axis=0)
    values = jnp.concatenate([kg_ref[ROWS : 2 * ROWS], rg_ref[ROWS : 2 * ROWS]], axis=0)
    for d, back in enumerate(back_refs):
        at = pl.ds(pl.multiple_of((2 * lax.rem(y + d, NY) + core) * PD, PD), PD)
        mine, other = kg_ref[at], rg_ref[at]
        first = core == 0
        back[0:PD] = jnp.where(first, mine, other)
        back[PD : 2 * PD] = jnp.where(first, other, mine)
    small = kg_ref[2 * ROWS :].astype(F32) + rg_ref[2 * ROWS :].astype(F32)
    flat = jnp.concatenate(
        [small[8 * g : 8 * g + 8] for g in range(9)] + [jnp.zeros((8, PLANE * SMALL - 9 * D), F32)], axis=1
    ).astype(BF16)
    proj_grad = tmm(cols[:, :512], rows)
    attn_grad = tmm(cols[:, 512:], values)
    for b in range(PLANE):
        groups = [proj_grad[32 * b + 8 * g : 32 * b + 8 * g + 8] for g in range(4)]
        groups += [attn_grad[24 * b + 8 * g : 24 * b + 8 * g + 8] for g in range(3)]
        for g, group in enumerate(groups):
            out_ref[b, :, g * D : (g + 1) * D] = group.astype(BF16)
        out_ref[b, :, 7 * D :] = flat[:, b * SMALL : (b + 1) * SMALL]


def back_kernel(p0_ref, p1_ref, p2_ref, p3_ref, proj_ref, out_ref, rows_ref):
    y = lax.axis_index("y")
    for d, piece in enumerate((p0_ref, p1_ref, p2_ref, p3_ref)):
        at = pl.ds(pl.multiple_of(lax.rem(y - d + NY, NY) * 2 * PD, 2 * PD), 2 * PD)
        rows_ref[at] = piece[...]
    out_ref[...] = mm_t(rows_ref[...], proj_ref[...]).astype(BF16)


def plane_kernel(in_ref, out_ref):
    total = in_ref[0].astype(F32)
    for s in range(1, PLANE):
        total = total + in_ref[s].astype(F32)
    proj = jnp.concatenate([total[:, g * D : (g + 1) * D] for g in range(4)], axis=0)
    attn = jnp.concatenate([total[:, g * D : (g + 1) * D] for g in range(4, 7)], axis=0)
    small = total[:, 7 * D :].astype(BF16)
    pad = jnp.zeros((1, D), F32)
    for z in range(NZ):
        own = jnp.concatenate([proj[4 * z : 4 * z + 4], attn[3 * z : 3 * z + 3], pad], axis=0)
        out_ref[z, :, :D] = own.astype(BF16)
        out_ref[z, :, D:] = small


def column_kernel(in_ref, proj_ref, attn_ref, small_ref):
    total = in_ref[0].astype(F32)
    for s in range(1, NZ):
        total = total + in_ref[s].astype(F32)
    proj_ref[...] = total[0:4, :D]
    attn_ref[...] = total[4:7, :D]
    mine = total[:, D:].astype(BF16)
    for s in range(PLANE):
        small_ref[s] = mine


def last_kernel(in_ref, head_ref, embed_ref, table_ref, loss_ref):
    got = jnp.concatenate([in_ref[b] for b in range(13)], axis=1).astype(F32)
    for g in range(4):
        head_ref[8 * g : 8 * g + 8] = got[:, g * D : (g + 1) * D]
        embed_ref[8 * g : 8 * g + 8] = got[:, (4 + g) * D : (5 + g) * D]
    tail = got[:, 8 * D :]
    table_ref[...] = jnp.concatenate([tail[:, 0:NIB], tail[:, LANES : LANES + NIB]], axis=0)
    loss_ref[...] = jnp.sum(tail[0:1, 2 * LANES : 3 * LANES], axis=1, keepdims=True) / TOTAL_BYTES


def call(kernel, outs, vmem=8, **more):
    return pl.pallas_call(
        kernel,
        out_shape=[jax.ShapeDtypeStruct(s, d) for s, d in outs],
        compiler_params=pltpu.CompilerParams(vmem_limit_bytes=vmem * 1024 * 1024),
        **more,
    )


def local(
    global_out, in_nibbles, target_nibbles, proj_weight, attn_weight, head_weight, byte_embed, lo_table
):
    plane = ("x", "y")
    swap = [(0, 1), (1, 0)]
    pos = lax.all_to_all(
        global_out.reshape(K, PD, DGT), ("y", "c"), split_axis=0, concat_axis=0, tiled=True
    ).reshape(ROWS, DGT)
    nibbles = jnp.concatenate([in_nibbles, target_nibbles], axis=0)
    nibbles = nibbles.transpose(0, 2, 1).reshape(4, ROWS)
    (proj_weight,) = call(
        fetch_kernel,
        [(proj_weight.shape, BF16)],
        in_specs=[pl.BlockSpec(memory_space=pl.ANY)],
        scratch_shapes=[pltpu.SemaphoreType.DMA],
    )(proj_weight)
    half = (ROWS, (DGT + D) // NC)
    local_spec = pl.BlockSpec(memory_space=pltpu.VMEM)
    grads, send_cols, keep_cols = call(
        main_kernel,
        [((GROWS, D), BF16), (half, BF16), (half, BF16)],
        52,
        in_specs=[local_spec] * 4 + [pl.BlockSpec(memory_space=pl.ANY)] + [local_spec] * 2,
        scratch_shapes=[pltpu.VMEM((4, D, D), BF16), pltpu.SemaphoreType.DMA((4,))],
    )(pos, nibbles, proj_weight, byte_embed, attn_weight, head_weight.T, lo_table.T)
    got_cols = lax.ppermute(send_cols, "c", swap)
    got_grads = lax.ppermute(grads, "c", swap)
    blocks, *back = call(pair_kernel, [((PLANE, 8, BLK), BF16)] + [((2 * PD, D), BF16)] * NY, 12)(
        keep_cols, got_cols, grads, got_grads
    )
    blocks = lax.all_to_all(blocks, plane, split_axis=0, concat_axis=0, tiled=True)
    (columns,) = call(plane_kernel, [((NZ, 8, D + SMALL), BF16)])(blocks)
    columns, *back = lax.optimization_barrier((columns, *back))
    columns = lax.all_to_all(columns, "z", split_axis=0, concat_axis=0, tiled=True)
    for d in range(1, NY):
        back[d] = lax.ppermute(back[d], "y", [(s, (s + d) % NY) for s in range(NY)])
    (grad_global,) = call(
        back_kernel, [((ROWS, DGT), BF16)], scratch_shapes=[pltpu.VMEM((ROWS, D), BF16)]
    )(*back, proj_weight)
    columns, grad_global = lax.optimization_barrier((columns, grad_global))
    grad_proj, grad_attn, small = call(
        column_kernel, [((4, D), F32), ((3, D), F32), ((PLANE, 8, SMALL), BF16)]
    )(columns)
    small = lax.all_to_all(small, plane, split_axis=0, concat_axis=0, tiled=True)
    head_rows, grad_embed, grad_table, loss = call(
        last_kernel,
        [((2 * NIB, D), F32), ((2 * NIB, D), F32), ((NIB, NIB), F32), ((1, 1), F32)],
    )(small)
    return (
        grad_global,
        grad_proj,
        grad_attn.reshape(3 * D),
        head_rows.T,
        grad_embed,
        grad_table,
        loss.reshape(()),
    )


def solution(mesh):
    axes = Mesh(mesh.devices.reshape(NX, NZ, NY, NC), ("x", "z", "y", "c"))
    every = ("x", "z", "y", "c")
    shard = P(("x", "z"), ("y", "c"))
    in_specs = (shard, P(None, every, None), P(None, every, None), P(), P(), P(), P(), P())
    out_specs = (shard, P(every, None), P(every), P(), P(), P(), P())
    return jax.shard_map(local, mesh=axes, in_specs=in_specs, out_specs=out_specs, check_vma=False)
```

```python
import jax
import jax.numpy as jnp
from jax import lax
from jax.experimental import pallas as pl
from jax.experimental.pallas import tpu as pltpu
from jax.sharding import Mesh, PartitionSpec as P

HEADS = 12
HS = 64
K = 8
PD = 16
ROWS = K * PD
D = 768
DGT = 1024
NIB = 16
LANES = 128
TILES = D // LANES
EPS = 1e-06
F32 = jnp.float32
BF16 = jnp.bfloat16
NX, NZ, NY, NC = 4, 8, 4, 2
PLANE = NX * NY
SMALL = 512
BLK = 7 * D + SMALL
GROWS = 336
TOTAL_BYTES = 32768


def mm(a, b):
    return jnp.dot(a, b, preferred_element_type=F32)


def mm_t(a, b):
    return lax.dot_general(a, b, (((1,), (1,)), ((), ())), preferred_element_type=F32)


def tmm(a, b, precision=None):
    return lax.dot_general(
        a, b, (((0,), (0,)), ((), ())), preferred_element_type=F32, precision=precision
    )


def norm_backward(values, inverse, upstream):
    summed = jnp.sum(upstream * values, axis=-1, keepdims=True) / D
    return inverse * (upstream - values * (inverse * inverse) * summed)


def owner_columns(size, piece, core):
    block = NZ * NY * NC * piece
    src = lax.broadcasted_iota(jnp.int32, (size, size), 0)
    dst = lax.broadcasted_iota(jnp.int32, (1, size), 1)
    half = dst // (size // 2)
    w = dst - half * (size // 2)
    xb = w // (block // 2)
    w = w - xb * (block // 2)
    y = w // (NZ * piece)
    w = w - y * (NZ * piece)
    z = w // piece
    i = w - z * piece
    c = jnp.where(half == 0, 1 - core, core)
    want = xb * block + z * (NY * NC * piece) + y * (NC * piece) + c * piece + i
    return (src == want).astype(BF16)


def softmax_cols(logits):
    e = jnp.exp(logits - jnp.max(logits, axis=0, keepdims=True))
    return e / jnp.sum(e, axis=0, keepdims=True)


def col_loss(logits, onehot):
    top = jnp.max(logits, axis=0, keepdims=True)
    total = jnp.sum(jnp.exp(logits - top), axis=0, keepdims=True)
    return top + jnp.log(total) - jnp.sum(logits * onehot, axis=0, keepdims=True)


def fetch_kernel(proj_hbm, proj_ref, sem):
    copy = pltpu.make_async_copy(proj_hbm, proj_ref, sem)
    copy.start()
    copy.wait()


def input_hot(nib_ref):
    codes = lax.broadcasted_iota(jnp.int32, (2 * NIB, ROWS), 0)
    return jnp.logical_or(codes == nib_ref[0:1, :], codes == nib_ref[1:2, :] + NIB).astype(BF16)


def main_kernel(
    pos_ref,
    nib_ref,
    proj_ref,
    embed_ref,
    attn_hbm,
    head_ref,
    lo_ref,
    out_ref,
    send_ref,
    keep_ref,
    attn_ref,
    sems,
):
    copies = [pltpu.make_async_copy(attn_hbm.at[w], attn_ref.at[w], sems.at[w]) for w in range(4)]
    for copy in copies:
        copy.start()
    core = lax.axis_index("c")
    pos = pos_ref[...]
    projected = mm(pos, proj_ref[...]).astype(BF16).astype(F32)
    in_hot = input_hot(nib_ref)
    state_in = projected + tmm(in_hot, embed_ref[...])
    inv_in = lax.rsqrt(jnp.mean(state_in * state_in, axis=-1, keepdims=True) + EPS)
    normed_in = (state_in * inv_in).astype(BF16)
    move = owner_columns(256, 4, core)
    for x in range(NX):
        cols = mm(pos[:, 256 * x : 256 * x + 256], move).astype(BF16)
        send_ref[:, 128 * x : 128 * x + 128] = cols[:, :128]
        keep_ref[:, 128 * x : 128 * x + 128] = cols[:, 128:]
    cols = mm(normed_in, owner_columns(D, 3, core)).astype(BF16)
    send_ref[:, 512:] = cols[:, : D // 2]
    keep_ref[:, 512:] = cols[:, D // 2 :]
    copies[0].wait()
    query = mm(normed_in, attn_ref[0]).astype(BF16)
    copies[1].wait()
    keys = mm(normed_in, attn_ref[1]).astype(BF16)
    copies[2].wait()
    values = mm(normed_in, attn_ref[2]).astype(BF16)

    key_row = lax.broadcasted_iota(jnp.int32, (ROWS, 2 * ROWS), 0)
    query_row = lax.broadcasted_iota(jnp.int32, (ROWS, 2 * ROWS), 1) % ROWS
    allowed = jnp.logical_and(key_row % PD == query_row % PD, key_row <= query_row)
    lane = lax.broadcasted_iota(jnp.int32, (2 * ROWS, LANES), 1)
    part = lax.broadcasted_iota(jnp.int32, (2 * ROWS, LANES), 0)
    own = ((lane // HS) == (part // ROWS)).astype(BF16)

    def two_heads(tile):
        return jnp.concatenate([tile, tile], axis=0) * own

    def stacked(cols):
        return jnp.concatenate([cols[:, :ROWS], cols[:, ROWS:]], axis=0)

    scale = 1.0 / HS**0.5
    probs, probs_low, contexts = [], [], []
    for t in range(TILES):
        cut = slice(t * LANES, (t + 1) * LANES)
        scores = mm_t(keys[:, cut], two_heads(query[:, cut])) * scale
        p = softmax_cols(jnp.where(allowed, scores, -1e30))
        low = p.astype(BF16)
        probs.append(p)
        probs_low.append(low)
        contexts.append(tmm(stacked(low), two_heads(values[:, cut])).astype(BF16))
    context = jnp.concatenate(contexts, axis=1)
    copies[3].wait()
    state_mid = state_in + mm(context, attn_ref[3])
    inv_mid = lax.rsqrt(jnp.mean(state_mid * state_mid, axis=-1, keepdims=True) + EPS)
    normed_mid = (state_mid * inv_mid).astype(BF16)

    logits = mm_t(head_ref[...], normed_mid)
    nib_codes = lax.broadcasted_iota(jnp.int32, (NIB, ROWS), 0)
    hi_hot = (nib_codes == nib_ref[2:3, :]).astype(F32)
    lo_hot = (nib_codes == nib_ref[3:4, :]).astype(F32)
    hi_logits = logits[:NIB]
    lo_logits = logits[NIB:] + jnp.dot(
        lo_ref[...], hi_hot, precision=lax.Precision.HIGHEST, preferred_element_type=F32
    )
    loss = col_loss(hi_logits, hi_hot) + col_loss(lo_logits, lo_hot)
    grad_hi = softmax_cols(hi_logits) - hi_hot
    grad_lo = softmax_cols(lo_logits) - lo_hot
    grad_table = lax.dot_general(
        hi_hot,
        jnp.concatenate([grad_lo, jnp.zeros((LANES - NIB, ROWS), F32)], axis=0),
        (((1,), (1,)), ((), ())),
        preferred_element_type=F32,
        precision=lax.Precision.HIGHEST,
    )
    grad_logits = jnp.concatenate([grad_hi, grad_lo], axis=0).astype(BF16)
    grad_head = mm(grad_logits, normed_mid)
    grad_mid = norm_backward(state_mid, inv_mid, tmm(grad_logits, head_ref[...]))
    grad_context = mm_t(grad_mid.astype(BF16), attn_ref[3]).astype(BF16)

    grad_q, grad_k, grad_v = [], [], []
    for t in range(TILES):
        cut = slice(t * LANES, (t + 1) * LANES)
        upstream = two_heads(grad_context[:, cut])
        grad_p = mm_t(values[:, cut], upstream)
        grad_v.append(mm(probs_low[t], upstream).astype(BF16))
        inner = jnp.sum(grad_p * probs[t], axis=0, keepdims=True)
        grad_s = (probs[t] * (grad_p - inner) * scale).astype(BF16)
        grad_k.append(mm(grad_s, two_heads(query[:, cut])).astype(BF16))
        grad_q.append(tmm(stacked(grad_s), two_heads(keys[:, cut])).astype(BF16))
    grad_values = jnp.concatenate(grad_v, axis=1)
    grad_normed = (
        mm_t(jnp.concatenate(grad_q, axis=1), attn_ref[0])
        + mm_t(jnp.concatenate(grad_k, axis=1), attn_ref[1])
        + mm_t(grad_values, attn_ref[2])
    )
    grad_in = grad_mid + norm_backward(state_in, inv_in, grad_normed)
    grad_rows = grad_in.astype(BF16)
    rest = (grad_in - grad_rows.astype(F32)).astype(BF16)
    grad_embed = mm(in_hot, grad_rows) + mm(in_hot, rest)

    out_ref[0:ROWS] = grad_rows
    out_ref[ROWS : 2 * ROWS] = grad_values
    tail = jnp.concatenate(
        [
            grad_table[:8],
            grad_table[8:],
            jnp.concatenate([loss, jnp.zeros((7, ROWS), F32)], axis=0),
            jnp.zeros((8, D - 3 * LANES), F32),
        ],
        axis=1,
    )
    out_ref[2 * ROWS : GROWS] = jnp.concatenate(
        [grad_head, grad_embed, tail, jnp.zeros((8, D), F32)], axis=0
    ).astype(BF16)


def pair_kernel(ka_ref, ra_ref, kg_ref, rg_ref, out_ref, *back_refs):
    core = lax.axis_index("c")
    y = lax.axis_index("y")
    cols = jnp.concatenate([ka_ref[...], ra_ref[...]], axis=0)
    rows = jnp.concatenate([kg_ref[0:ROWS], rg_ref[0:ROWS]], axis=0)
    values = jnp.concatenate([kg_ref[ROWS : 2 * ROWS], rg_ref[ROWS : 2 * ROWS]], axis=0)
    for d, back in enumerate(back_refs):
        at = pl.ds(pl.multiple_of((2 * lax.rem(y + d, NY) + core) * PD, PD), PD)
        mine, other = kg_ref[at], rg_ref[at]
        first = core == 0
        back[0:PD] = jnp.where(first, mine, other)
        back[PD : 2 * PD] = jnp.where(first, other, mine)
    small = kg_ref[2 * ROWS :].astype(F32) + rg_ref[2 * ROWS :].astype(F32)
    flat = jnp.concatenate(
        [small[8 * g : 8 * g + 8] for g in range(9)] + [jnp.zeros((8, PLANE * SMALL - 9 * D), F32)], axis=1
    ).astype(BF16)
    proj_grad = tmm(cols[:, :512], rows)
    attn_grad = tmm(cols[:, 512:], values)
    for b in range(PLANE):
        groups = [proj_grad[32 * b + 8 * g : 32 * b + 8 * g + 8] for g in range(4)]
        groups += [attn_grad[24 * b + 8 * g : 24 * b + 8 * g + 8] for g in range(3)]
        for g, group in enumerate(groups):
            out_ref[b, :, g * D : (g + 1) * D] = group.astype(BF16)
        out_ref[b, :, 7 * D :] = flat[:, b * SMALL : (b + 1) * SMALL]


def back_kernel(p0_ref, p1_ref, p2_ref, p3_ref, proj_ref, out_ref, rows_ref):
    y = lax.axis_index("y")
    for d, piece in enumerate((p0_ref, p1_ref, p2_ref, p3_ref)):
        at = pl.ds(pl.multiple_of(lax.rem(y - d + NY, NY) * 2 * PD, 2 * PD), 2 * PD)
        rows_ref[at] = piece[...]
    out_ref[...] = mm_t(rows_ref[...], proj_ref[...]).astype(BF16)


def plane_kernel(in_ref, out_ref):
    total = in_ref[0].astype(F32)
    for s in range(1, PLANE):
        total = total + in_ref[s].astype(F32)
    proj = jnp.concatenate([total[:, g * D : (g + 1) * D] for g in range(4)], axis=0)
    attn = jnp.concatenate([total[:, g * D : (g + 1) * D] for g in range(4, 7)], axis=0)
    small = total[:, 7 * D :].astype(BF16)
    pad = jnp.zeros((1, D), F32)
    for z in range(NZ):
        own = jnp.concatenate([proj[4 * z : 4 * z + 4], attn[3 * z : 3 * z + 3], pad], axis=0)
        out_ref[z, :, :D] = own.astype(BF16)
        out_ref[z, :, D:] = small


def column_kernel(in_ref, proj_ref, attn_ref, small_ref):
    total = in_ref[0].astype(F32)
    for s in range(1, NZ):
        total = total + in_ref[s].astype(F32)
    proj_ref[...] = total[0:4, :D]
    attn_ref[...] = total[4:7, :D]
    mine = total[:, D:].astype(BF16)
    for s in range(PLANE):
        small_ref[s] = mine


def last_kernel(in_ref, head_ref, embed_ref, table_ref, loss_ref):
    got = jnp.concatenate([in_ref[b] for b in range(13)], axis=1).astype(F32)
    for g in range(4):
        head_ref[8 * g : 8 * g + 8] = got[:, g * D : (g + 1) * D]
        embed_ref[8 * g : 8 * g + 8] = got[:, (4 + g) * D : (5 + g) * D]
    tail = got[:, 8 * D :]
    table_ref[...] = jnp.concatenate([tail[:, 0:NIB], tail[:, LANES : LANES + NIB]], axis=0)
    loss_ref[...] = jnp.sum(tail[0:1, 2 * LANES : 3 * LANES], axis=1, keepdims=True) / TOTAL_BYTES


def call(kernel, outs, vmem=8, **more):
    return pl.pallas_call(
        kernel,
        out_shape=[jax.ShapeDtypeStruct(s, d) for s, d in outs],
        compiler_params=pltpu.CompilerParams(vmem_limit_bytes=vmem * 1024 * 1024),
        **more,
    )


def local(
    global_out, in_nibbles, target_nibbles, proj_weight, attn_weight, head_weight, byte_embed, lo_table
):
    plane = ("x", "y")
    swap = [(0, 1), (1, 0)]
    pos = lax.all_to_all(
        global_out.reshape(K, PD, DGT), ("y", "c"), split_axis=0, concat_axis=0, tiled=True
    ).reshape(ROWS, DGT)
    nibbles = jnp.concatenate([in_nibbles, target_nibbles], axis=0)
    nibbles = nibbles.transpose(0, 2, 1).reshape(4, ROWS)
    (proj_weight,) = call(
        fetch_kernel,
        [(proj_weight.shape, BF16)],
        in_specs=[pl.BlockSpec(memory_space=pl.ANY)],
        scratch_shapes=[pltpu.SemaphoreType.DMA],
    )(proj_weight)
    half = (ROWS, (DGT + D) // NC)
    local_spec = pl.BlockSpec(memory_space=pltpu.VMEM)
    grads, send_cols, keep_cols = call(
        main_kernel,
        [((GROWS, D), BF16), (half, BF16), (half, BF16)],
        50,
        in_specs=[local_spec] * 4 + [pl.BlockSpec(memory_space=pl.ANY)] + [local_spec] * 2,
        scratch_shapes=[pltpu.VMEM((4, D, D), BF16), pltpu.SemaphoreType.DMA((4,))],
    )(pos, nibbles, proj_weight, byte_embed, attn_weight, head_weight.T, lo_table.T)
    got_cols = lax.ppermute(send_cols, "c", swap)
    got_grads = lax.ppermute(grads, "c", swap)
    blocks, *back = call(pair_kernel, [((PLANE, 8, BLK), BF16)] + [((2 * PD, D), BF16)] * NY, 12)(
        keep_cols, got_cols, grads, got_grads
    )
    blocks = lax.all_to_all(blocks, plane, split_axis=0, concat_axis=0, tiled=True)
    (columns,) = call(plane_kernel, [((NZ, 8, D + SMALL), BF16)])(blocks)
    columns, *back = lax.optimization_barrier((columns, *back))
    columns = lax.all_to_all(columns, "z", split_axis=0, concat_axis=0, tiled=True)
    for d in range(1, NY):
        back[d] = lax.ppermute(back[d], "y", [(s, (s + d) % NY) for s in range(NY)])
    (grad_global,) = call(
        back_kernel, [((ROWS, DGT), BF16)], scratch_shapes=[pltpu.VMEM((ROWS, D), BF16)]
    )(*back, proj_weight)
    columns, grad_global = lax.optimization_barrier((columns, grad_global))
    grad_proj, grad_attn, small = call(
        column_kernel, [((4, D), F32), ((3, D), F32), ((PLANE, 8, SMALL), BF16)]
    )(columns)
    small = lax.all_to_all(small, plane, split_axis=0, concat_axis=0, tiled=True)
    head_rows, grad_embed, grad_table, loss = call(
        last_kernel,
        [((2 * NIB, D), F32), ((2 * NIB, D), F32), ((NIB, NIB), F32), ((1, 1), F32)],
    )(small)
    return (
        grad_global,
        grad_proj,
        grad_attn.reshape(3 * D),
        head_rows.T,
        grad_embed,
        grad_table,
        loss.reshape(()),
    )


def solution(mesh):
    axes = Mesh(mesh.devices.reshape(NX, NZ, NY, NC), ("x", "z", "y", "c"))
    every = ("x", "z", "y", "c")
    shard = P(("x", "z"), ("y", "c"))
    in_specs = (shard, P(None, every, None), P(None, every, None), P(), P(), P(), P(), P())
    out_specs = (shard, P(every, None), P(every), P(), P(), P(), P())
    return jax.shard_map(local, mesh=axes, in_specs=in_specs, out_specs=out_specs, check_vma=False)
```

```python
import jax
import jax.numpy as jnp
from jax import lax
from jax.experimental import pallas as pl
from jax.experimental.pallas import tpu as pltpu
from jax.sharding import Mesh, PartitionSpec as P

HEADS = 12
HS = 64
K = 8
PD = 16
ROWS = K * PD
D = 768
DGT = 1024
NIB = 16
LANES = 128
TILES = D // LANES
EPS = 1e-06
F32 = jnp.float32
BF16 = jnp.bfloat16
NX, NZ, NY, NC = 4, 8, 4, 2
PLANE = NX * NY
SMALL = 512
BLK = 7 * D + SMALL
GROWS = 336
TOTAL_BYTES = 32768


def mm(a, b):
    return jnp.dot(a, b, preferred_element_type=F32)


def mm_t(a, b):
    return lax.dot_general(a, b, (((1,), (1,)), ((), ())), preferred_element_type=F32)


def tmm(a, b, precision=None):
    return lax.dot_general(
        a, b, (((0,), (0,)), ((), ())), preferred_element_type=F32, precision=precision
    )


def norm_backward(values, inverse, upstream):
    summed = jnp.sum(upstream * values, axis=-1, keepdims=True) / D
    return inverse * (upstream - values * (inverse * inverse) * summed)


def owner_columns(size, piece, core):
    block = NZ * NY * NC * piece
    src = lax.broadcasted_iota(jnp.int32, (size, size), 0)
    dst = lax.broadcasted_iota(jnp.int32, (1, size), 1)
    half = dst // (size // 2)
    w = dst - half * (size // 2)
    xb = w // (block // 2)
    w = w - xb * (block // 2)
    y = w // (NZ * piece)
    w = w - y * (NZ * piece)
    z = w // piece
    i = w - z * piece
    c = jnp.where(half == 0, 1 - core, core)
    want = xb * block + z * (NY * NC * piece) + y * (NC * piece) + c * piece + i
    return (src == want).astype(BF16)


def softmax_cols(logits):
    e = jnp.exp(logits - jnp.max(logits, axis=0, keepdims=True))
    return e / jnp.sum(e, axis=0, keepdims=True)


def col_loss(logits, onehot):
    top = jnp.max(logits, axis=0, keepdims=True)
    total = jnp.sum(jnp.exp(logits - top), axis=0, keepdims=True)
    return top + jnp.log(total) - jnp.sum(logits * onehot, axis=0, keepdims=True)


def fetch_kernel(proj_hbm, proj_ref, sem):
    copy = pltpu.make_async_copy(proj_hbm, proj_ref, sem)
    copy.start()
    copy.wait()


def input_hot(nib_ref):
    codes = lax.broadcasted_iota(jnp.int32, (2 * NIB, ROWS), 0)
    return jnp.logical_or(codes == nib_ref[0:1, :], codes == nib_ref[1:2, :] + NIB).astype(BF16)


def main_kernel(
    pos_ref,
    nib_ref,
    proj_ref,
    embed_ref,
    attn_hbm,
    head_ref,
    lo_ref,
    out_ref,
    send_ref,
    keep_ref,
    attn_ref,
    sems,
):
    copies = [pltpu.make_async_copy(attn_hbm.at[w], attn_ref.at[w], sems.at[w]) for w in range(4)]
    for copy in copies:
        copy.start()
    core = lax.axis_index("c")
    pos = pos_ref[...]
    projected = mm(pos, proj_ref[...]).astype(BF16).astype(F32)
    in_hot = input_hot(nib_ref)
    state_in = projected + tmm(in_hot, embed_ref[...])
    inv_in = lax.rsqrt(jnp.mean(state_in * state_in, axis=-1, keepdims=True) + EPS)
    normed_in = (state_in * inv_in).astype(BF16)
    move = owner_columns(256, 4, core)
    for x in range(NX):
        cols = mm(pos[:, 256 * x : 256 * x + 256], move).astype(BF16)
        send_ref[:, 128 * x : 128 * x + 128] = cols[:, :128]
        keep_ref[:, 128 * x : 128 * x + 128] = cols[:, 128:]
    cols = mm(normed_in, owner_columns(D, 3, core)).astype(BF16)
    send_ref[:, 512:] = cols[:, : D // 2]
    keep_ref[:, 512:] = cols[:, D // 2 :]
    copies[0].wait()
    query = mm(normed_in, attn_ref[0]).astype(BF16)
    copies[1].wait()
    keys = mm(normed_in, attn_ref[1]).astype(BF16)
    copies[2].wait()
    values = mm(normed_in, attn_ref[2]).astype(BF16)

    key_row = lax.broadcasted_iota(jnp.int32, (ROWS, 2 * ROWS), 0)
    query_row = lax.broadcasted_iota(jnp.int32, (ROWS, 2 * ROWS), 1) % ROWS
    allowed = jnp.logical_and(key_row % PD == query_row % PD, key_row <= query_row)
    lane = lax.broadcasted_iota(jnp.int32, (2 * ROWS, LANES), 1)
    part = lax.broadcasted_iota(jnp.int32, (2 * ROWS, LANES), 0)
    own = ((lane // HS) == (part // ROWS)).astype(BF16)

    def two_heads(tile):
        return jnp.concatenate([tile, tile], axis=0) * own

    def stacked(cols):
        return jnp.concatenate([cols[:, :ROWS], cols[:, ROWS:]], axis=0)

    scale = 1.0 / HS**0.5
    probs, probs_low, contexts = [], [], []
    for t in range(TILES):
        cut = slice(t * LANES, (t + 1) * LANES)
        scores = mm_t(keys[:, cut], two_heads(query[:, cut])) * scale
        p = softmax_cols(jnp.where(allowed, scores, -1e30))
        low = p.astype(BF16)
        probs.append(p)
        probs_low.append(low)
        contexts.append(tmm(stacked(low), two_heads(values[:, cut])).astype(BF16))
    context = jnp.concatenate(contexts, axis=1)
    copies[3].wait()
    state_mid = state_in + mm(context, attn_ref[3])
    inv_mid = lax.rsqrt(jnp.mean(state_mid * state_mid, axis=-1, keepdims=True) + EPS)
    normed_mid = (state_mid * inv_mid).astype(BF16)

    logits = mm_t(head_ref[...], normed_mid)
    nib_codes = lax.broadcasted_iota(jnp.int32, (NIB, ROWS), 0)
    hi_hot = (nib_codes == nib_ref[2:3, :]).astype(F32)
    lo_hot = (nib_codes == nib_ref[3:4, :]).astype(F32)
    hi_logits = logits[:NIB]
    lo_logits = logits[NIB:] + jnp.dot(
        lo_ref[...], hi_hot, precision=lax.Precision.HIGHEST, preferred_element_type=F32
    )
    loss = col_loss(hi_logits, hi_hot) + col_loss(lo_logits, lo_hot)
    grad_hi = softmax_cols(hi_logits) - hi_hot
    grad_lo = softmax_cols(lo_logits) - lo_hot
    grad_table = lax.dot_general(
        hi_hot,
        jnp.concatenate([grad_lo, jnp.zeros((LANES - NIB, ROWS), F32)], axis=0),
        (((1,), (1,)), ((), ())),
        preferred_element_type=F32,
        precision=lax.Precision.HIGHEST,
    )
    grad_logits = jnp.concatenate([grad_hi, grad_lo], axis=0).astype(BF16)
    grad_head = mm(grad_logits, normed_mid)
    grad_mid = norm_backward(state_mid, inv_mid, tmm(grad_logits, head_ref[...]))
    grad_context = mm_t(grad_mid.astype(BF16), attn_ref[3]).astype(BF16)

    grad_q, grad_k, grad_v = [], [], []
    for t in range(TILES):
        cut = slice(t * LANES, (t + 1) * LANES)
        upstream = two_heads(grad_context[:, cut])
        grad_p = mm_t(values[:, cut], upstream)
        grad_v.append(mm(probs_low[t], upstream).astype(BF16))
        inner = jnp.sum(grad_p * probs[t], axis=0, keepdims=True)
        grad_s = (probs[t] * (grad_p - inner) * scale).astype(BF16)
        grad_k.append(mm(grad_s, two_heads(query[:, cut])).astype(BF16))
        grad_q.append(tmm(stacked(grad_s), two_heads(keys[:, cut])).astype(BF16))
    grad_values = jnp.concatenate(grad_v, axis=1)
    grad_normed = (
        mm_t(jnp.concatenate(grad_q, axis=1), attn_ref[0])
        + mm_t(jnp.concatenate(grad_k, axis=1), attn_ref[1])
        + mm_t(grad_values, attn_ref[2])
    )
    grad_in = grad_mid + norm_backward(state_in, inv_in, grad_normed)
    grad_rows = grad_in.astype(BF16)
    rest = (grad_in - grad_rows.astype(F32)).astype(BF16)
    grad_embed = mm(in_hot, grad_rows) + mm(in_hot, rest)

    out_ref[0:ROWS] = grad_rows
    out_ref[ROWS : 2 * ROWS] = grad_values
    tail = jnp.concatenate(
        [
            grad_table[:8],
            grad_table[8:],
            jnp.concatenate([loss, jnp.zeros((7, ROWS), F32)], axis=0),
            jnp.zeros((8, D - 3 * LANES), F32),
        ],
        axis=1,
    )
    out_ref[2 * ROWS : GROWS] = jnp.concatenate(
        [grad_head, grad_embed, tail, jnp.zeros((8, D), F32)], axis=0
    ).astype(BF16)


def pair_kernel(ka_ref, ra_ref, kg_ref, rg_ref, out_ref, *back_refs):
    core = lax.axis_index("c")
    y = lax.axis_index("y")
    cols = jnp.concatenate([ka_ref[...], ra_ref[...]], axis=0)
    rows = jnp.concatenate([kg_ref[0:ROWS], rg_ref[0:ROWS]], axis=0)
    values = jnp.concatenate([kg_ref[ROWS : 2 * ROWS], rg_ref[ROWS : 2 * ROWS]], axis=0)
    for d, back in enumerate(back_refs):
        at = pl.ds(pl.multiple_of((2 * lax.rem(y + d, NY) + core) * PD, PD), PD)
        mine, other = kg_ref[at], rg_ref[at]
        first = core == 0
        back[0:PD] = jnp.where(first, mine, other)
        back[PD : 2 * PD] = jnp.where(first, other, mine)
    small = kg_ref[2 * ROWS :].astype(F32) + rg_ref[2 * ROWS :].astype(F32)
    flat = jnp.concatenate(
        [small[8 * g : 8 * g + 8] for g in range(9)] + [jnp.zeros((8, PLANE * SMALL - 9 * D), F32)], axis=1
    ).astype(BF16)
    proj_grad = tmm(cols[:, :512], rows)
    attn_grad = tmm(cols[:, 512:], values)
    for b in range(PLANE):
        groups = [proj_grad[32 * b + 8 * g : 32 * b + 8 * g + 8] for g in range(4)]
        groups += [attn_grad[24 * b + 8 * g : 24 * b + 8 * g + 8] for g in range(3)]
        for g, group in enumerate(groups):
            out_ref[b, :, g * D : (g + 1) * D] = group.astype(BF16)
        out_ref[b, :, 7 * D :] = flat[:, b * SMALL : (b + 1) * SMALL]


def back_kernel(p0_ref, p1_ref, p2_ref, p3_ref, proj_ref, out_ref, rows_ref):
    y = lax.axis_index("y")
    for d, piece in enumerate((p0_ref, p1_ref, p2_ref, p3_ref)):
        at = pl.ds(pl.multiple_of(lax.rem(y - d + NY, NY) * 2 * PD, 2 * PD), 2 * PD)
        rows_ref[at] = piece[...]
    out_ref[...] = mm_t(rows_ref[...], proj_ref[...]).astype(BF16)


def plane_kernel(in_ref, out_ref):
    total = in_ref[0].astype(F32)
    for s in range(1, PLANE):
        total = total + in_ref[s].astype(F32)
    proj = jnp.concatenate([total[:, g * D : (g + 1) * D] for g in range(4)], axis=0)
    attn = jnp.concatenate([total[:, g * D : (g + 1) * D] for g in range(4, 7)], axis=0)
    small = total[:, 7 * D :].astype(BF16)
    pad = jnp.zeros((1, D), F32)
    for z in range(NZ):
        own = jnp.concatenate([proj[4 * z : 4 * z + 4], attn[3 * z : 3 * z + 3], pad], axis=0)
        out_ref[z, :, :D] = own.astype(BF16)
        out_ref[z, :, D:] = small


def small_kernel(in_ref, small_ref):
    total = in_ref[0, :, D:].astype(F32)
    for s in range(1, NZ):
        total = total + in_ref[s, :, D:].astype(F32)
    mine = total.astype(BF16)
    for s in range(PLANE):
        small_ref[s] = mine


def column_kernel(in_ref, proj_ref, attn_ref):
    total = in_ref[0, :, :D].astype(F32)
    for s in range(1, NZ):
        total = total + in_ref[s, :, :D].astype(F32)
    proj_ref[...] = total[0:4]
    attn_ref[...] = total[4:7]


def last_kernel(in_ref, head_ref, embed_ref, table_ref, loss_ref):
    got = jnp.concatenate([in_ref[b] for b in range(13)], axis=1).astype(F32)
    for g in range(4):
        head_ref[8 * g : 8 * g + 8] = got[:, g * D : (g + 1) * D]
        embed_ref[8 * g : 8 * g + 8] = got[:, (4 + g) * D : (5 + g) * D]
    tail = got[:, 8 * D :]
    table_ref[...] = jnp.concatenate([tail[:, 0:NIB], tail[:, LANES : LANES + NIB]], axis=0)
    loss_ref[...] = jnp.sum(tail[0:1, 2 * LANES : 3 * LANES], axis=1, keepdims=True) / TOTAL_BYTES


def call(kernel, outs, vmem=8, **more):
    return pl.pallas_call(
        kernel,
        out_shape=[jax.ShapeDtypeStruct(s, d) for s, d in outs],
        compiler_params=pltpu.CompilerParams(vmem_limit_bytes=vmem * 1024 * 1024),
        **more,
    )


def local(
    global_out, in_nibbles, target_nibbles, proj_weight, attn_weight, head_weight, byte_embed, lo_table
):
    plane = ("x", "y")
    swap = [(0, 1), (1, 0)]
    pos = lax.all_to_all(
        global_out.reshape(K, PD, DGT), ("y", "c"), split_axis=0, concat_axis=0, tiled=True
    ).reshape(ROWS, DGT)
    nibbles = jnp.concatenate([in_nibbles, target_nibbles], axis=0)
    nibbles = nibbles.transpose(0, 2, 1).reshape(4, ROWS)
    (proj_weight,) = call(
        fetch_kernel,
        [(proj_weight.shape, BF16)],
        in_specs=[pl.BlockSpec(memory_space=pl.ANY)],
        scratch_shapes=[pltpu.SemaphoreType.DMA],
    )(proj_weight)
    half = (ROWS, (DGT + D) // NC)
    local_spec = pl.BlockSpec(memory_space=pltpu.VMEM)
    grads, send_cols, keep_cols = call(
        main_kernel,
        [((GROWS, D), BF16), (half, BF16), (half, BF16)],
        50,
        in_specs=[local_spec] * 4 + [pl.BlockSpec(memory_space=pl.ANY)] + [local_spec] * 2,
        scratch_shapes=[pltpu.VMEM((4, D, D), BF16), pltpu.SemaphoreType.DMA((4,))],
    )(pos, nibbles, proj_weight, byte_embed, attn_weight, head_weight.T, lo_table.T)
    got_cols = lax.ppermute(send_cols, "c", swap)
    got_grads = lax.ppermute(grads, "c", swap)
    blocks, *back = call(pair_kernel, [((PLANE, 8, BLK), BF16)] + [((2 * PD, D), BF16)] * NY, 12)(
        keep_cols, got_cols, grads, got_grads
    )
    blocks = lax.all_to_all(blocks, plane, split_axis=0, concat_axis=0, tiled=True)
    (columns,) = call(plane_kernel, [((NZ, 8, D + SMALL), BF16)])(blocks)
    columns, *back = lax.optimization_barrier((columns, *back))
    columns = lax.all_to_all(columns, "z", split_axis=0, concat_axis=0, tiled=True)
    for d in range(1, NY):
        back[d] = lax.ppermute(back[d], "y", [(s, (s + d) % NY) for s in range(NY)])
    (grad_global,) = call(
        back_kernel, [((ROWS, DGT), BF16)], scratch_shapes=[pltpu.VMEM((ROWS, D), BF16)]
    )(*back, proj_weight)
    columns, grad_global = lax.optimization_barrier((columns, grad_global))
    (small,) = call(small_kernel, [((PLANE, 8, SMALL), BF16)])(columns)
    grad_proj, grad_attn = call(column_kernel, [((4, D), F32), ((3, D), F32)])(columns)
    small = lax.all_to_all(small, plane, split_axis=0, concat_axis=0, tiled=True)
    head_rows, grad_embed, grad_table, loss = call(
        last_kernel,
        [((2 * NIB, D), F32), ((2 * NIB, D), F32), ((NIB, NIB), F32), ((1, 1), F32)],
    )(small)
    return (
        grad_global,
        grad_proj,
        grad_attn.reshape(3 * D),
        head_rows.T,
        grad_embed,
        grad_table,
        loss.reshape(()),
    )


def solution(mesh):
    axes = Mesh(mesh.devices.reshape(NX, NZ, NY, NC), ("x", "z", "y", "c"))
    every = ("x", "z", "y", "c")
    shard = P(("x", "z"), ("y", "c"))
    in_specs = (shard, P(None, every, None), P(None, every, None), P(), P(), P(), P(), P())
    out_specs = (shard, P(every, None), P(every), P(), P(), P(), P())
    return jax.shard_map(local, mesh=axes, in_specs=in_specs, out_specs=out_specs, check_vma=False)
```
